256 devices in a mesh: dp: 4 (over y), expert: 64 (over z, x, core).
Axes of the slice: x: 4, y: 4, z: 8, core: 2. Of those that a mesh axis runs over, the one named last changes fastest.
Arguments:
- out_grad: bfloat16 [4, 8192, 4096], P('dp', 'expert'), may hold values from -6 to 6
- count: int32 [4, 8192], P('dp', 'expert'), may hold values from 0 to 64, as said below
- chosen: int32 [4, 128, 128], P('dp', 'expert'), may hold values from 0 to 8191, as said below
- gates: float32 [4, 128, 128], P('dp', 'expert'), may hold values from 0.1 to 1
- x_slots: bfloat16 [4, 128, 128, 4096], P('dp', 'expert'), may hold values from -6 to 6
- w_in: bfloat16 [128, 4096, 512], P('expert', None, 'dp'), may hold values from -0.09375 to 0.09375
- w_out: bfloat16 [128, 512, 4096], P('expert', 'dp'), may hold values from -0.25 to 0.25
Outputs:
- token_grad: bfloat16 [4, 8192, 4096], P('dp', 'expert')
- gate_grad: float32 [4, 128, 128], P('dp', 'expert')
- w_in_grad: bfloat16 [128, 4096, 512], P('expert', None, 'dp')
- w_out_grad: bfloat16 [128, 512, 4096], P('expert', 'dp')
The draws below stay inside these ranges and needn't reach their ends.
Inputs may be any that keep to these rules, and one draw needn't show every extreme that they name: `chosen`: in each group, one expert's 128 slots name different tokens, and one device's 2 experts together name different tokens. Within a group, the slots of one device's experts name at most 6 tokens of any one device (device j of expert holds the group's tokens j * 128 to (j + 1) * 128 - 1), and every such device's experts name exactly 6 tokens of some device. count[g,t] is the number of slots of group g, over all experts, whose chosen token is t; each device of expert contributes at most one.
All inputs are finite; a program needn't handle non-finite values.
Results may differ from the reference program's by a relative error of at most 0.007.
Values may be sent and summed in bfloat16 or wider, within the bound.
No kernel may reach another device: no remote copies, remote signals or barrier semaphores. Data moves between devices by JAX's collectives and lax.ppermute only.
A program may use at most 128 MiB of HBM per device.

```python
import math
import jax
import jax.numpy as jnp
from jax import lax

D = 4096
FF = 512
EXP_DEV = 2
TOK_DEV = 128
EXPERTS = 128
TOK_GROUP = 8192
CAP = 128
PEER = 6
N_DP = 4
N_EXPERT = 64


def route_tables(key):
    slots = EXP_DEV * CAP
    key_shared, key_owners = jax.random.split(key)
    shared_rows = jax.random.randint(key_shared, (N_DP, N_EXPERT), 0, TOK_DEV)
    owner_keys = jax.random.split(key_owners, N_DP * N_EXPERT)
    group_of_owner = jnp.arange(N_DP * N_EXPERT, dtype=jnp.int32) // N_EXPERT

    def one_owner(owner_key, group_index):
        key_order, key_offset, key_shuffle = jax.random.split(owner_key, 3)
        source_order = jax.random.permutation(key_order, N_EXPERT)
        hot_source = source_order[0]
        cold_sources = source_order[1:]
        slot_ids = jnp.arange(slots, dtype=jnp.int32)
        later = jnp.maximum(slot_ids - PEER, 0)
        source = jnp.where(slot_ids < PEER, hot_source, cold_sources[later % (N_EXPERT - 1)])
        slot_rank = jnp.where(slot_ids < PEER, slot_ids, later // (N_EXPERT - 1))
        offsets = jax.random.randint(key_offset, (N_EXPERT,), 0, TOK_DEV - 1)
        base_row = shared_rows[group_index][source]
        step_row = (jnp.maximum(slot_rank - 1, 0) + offsets[source]) % (TOK_DEV - 1) + 1
        local_row = jnp.where(slot_rank == 0, base_row, (base_row + step_row) % TOK_DEV)
        token_ids = source * TOK_DEV + local_row
        shuffle = jax.random.permutation(key_shuffle, slots)
        return token_ids[shuffle].reshape(EXP_DEV, CAP)
    tables = jax.vmap(one_owner)(owner_keys, group_of_owner)
    return tables.reshape(N_DP, N_EXPERT * EXP_DEV, CAP).astype(jnp.int32)


def token_counts(tables):
    group_ids = jnp.broadcast_to(jnp.arange(N_DP, dtype=jnp.int32)[:, None, None], tables.shape)
    totals = jnp.zeros((N_DP, TOK_GROUP), jnp.int32)
    return totals.at[group_ids.reshape(-1), tables.reshape(-1)].add(1)


def draw_chosen(key, part):
    tables = route_tables(key)
    return tables


def draw_count(key, part):
    tables = route_tables(key)
    return token_counts(tables)


def draw_out_grad(key, part):
    totals = token_counts(route_tables(key))
    key = jax.random.fold_in(key, 7)
    key_base, key_size = jax.random.split(key)
    shape = (N_DP, TOK_GROUP, D)
    base = jax.random.truncated_normal(key_base, -6.0, 6.0, shape, jnp.float32)
    magnitude = jax.random.uniform(key_size, shape, jnp.float32, 3.0, 6.0)
    strong = jnp.where(base >= 0.0, magnitude, -magnitude)
    popular = (2 * totals >= N_EXPERT)[:, :, None]
    return jnp.where(popular, strong, base).astype(jnp.bfloat16)


def block_scale(key, dims, cuts, low, top_value):
    level = 1.0
    for position, blocks in cuts:
        heights = jax.random.uniform(jax.random.fold_in(jax.random.fold_in(key, 6), position), (blocks,), jnp.float32, low / len(cuts), top_value / len(cuts))
        level = level * jnp.repeat(jnp.exp(heights), dims[position] // blocks).reshape((-1,) + (1,) * (len(dims) - 1 - position))
    return level


def scatter_about(rng, extent, scale, limit, pieces=(), kind=jnp.bfloat16):
    entries = scale * jax.random.normal(rng, extent, jnp.float32)
    if pieces:
        entries = entries * block_scale(rng, extent, pieces, -0.22, 0.18)
    return jnp.clip(entries, -limit, limit).astype(kind)


def setup_inputs(seed: int = 0) -> dict:
    splits = jax.random.split(jax.random.key(seed), 8)
    out_grad = draw_out_grad(jax.random.fold_in(splits[7], 71), 0)
    count = draw_count(jax.random.fold_in(splits[7], 71), 0)
    chosen = draw_chosen(jax.random.fold_in(splits[7], 71), 0)
    gates = jnp.clip(jnp.exp(math.log(1.0) - 2.3025851 * jax.random.uniform(splits[3], (N_DP, EXPERTS, CAP), jnp.float32) ** block_scale(splits[3], (N_DP, EXPERTS, CAP), ((0, 4), (1, 64)), -0.2, 0.2)), 0.1, 1.0)
    x_slots = scatter_about(splits[4], (N_DP, EXPERTS, CAP, D), 1.0, 6.0, ((0, 4), (1, 64)))
    w_in = scatter_about(splits[5], (EXPERTS, D, FF), D ** -0.5, 0.09375, ((0, 64), (2, 4)))
    w_out = scatter_about(splits[6], (EXPERTS, FF, D), FF ** -0.5, 0.25, ((0, 64), (1, 4)))
    return {"out_grad": out_grad, "count": count, "chosen": chosen, "gates": gates, "x_slots": x_slots, "w_in": w_in, "w_out": w_out}


SQRT_HALF = 0.7071067811865476
INV_ROOT_TWO_PI = 0.3989422804014327


def activation(pre):
    normal_cdf = 0.5 * (1.0 + lax.erf(pre * SQRT_HALF))
    slope = normal_cdf + pre * jnp.exp(-0.5 * pre * pre) * INV_ROOT_TWO_PI
    return pre * normal_cdf, slope


def pick_rows(table, token_ids):
    return table[token_ids]


def reference(out_grad, count, chosen, gates, x_slots, w_in, w_out):
    groups = out_grad.shape[0]
    width = out_grad.shape[2]

    def per_expert(items):
        token_ids, gate_e, inputs, proj_in, proj_out = items
        upstream = jax.vmap(pick_rows)(out_grad, token_ids)
        slot_count = jax.vmap(pick_rows)(count, token_ids).astype(jnp.float32).reshape(-1)
        scale_flat = gate_e.reshape(-1) / slot_count
        rows_per = inputs.shape[1]
        flat_in = inputs.reshape(-1, width)
        flat_up = upstream.reshape(-1, width)
        pre = jnp.dot(flat_in, proj_in, preferred_element_type=jnp.float32)
        hidden_f, slope = activation(pre)
        hidden = hidden_f.astype(jnp.bfloat16)
        project = jnp.dot(flat_up, proj_out.T, preferred_element_type=jnp.float32)
        gate_part = jnp.sum(hidden.astype(jnp.float32) * project, axis=1) / slot_count
        pre_grad = (scale_flat[:, None] * project * slope).astype(jnp.bfloat16)
        out_slot = (scale_flat[:, None] * flat_up.astype(jnp.float32)).astype(jnp.bfloat16)
        back_part = jnp.dot(pre_grad, proj_in.T, preferred_element_type=jnp.float32).astype(jnp.bfloat16)
        grad_in = jnp.zeros(proj_in.shape, jnp.float32)
        grad_out = jnp.zeros(proj_out.shape, jnp.float32)
        for group in range(groups):
            low = group * rows_per
            high = low + rows_per
            term_in = jnp.dot(flat_in[low:high].T, pre_grad[low:high], preferred_element_type=jnp.float32)
            term_out = jnp.dot(hidden[low:high].T, out_slot[low:high], preferred_element_type=jnp.float32)
            grad_in = grad_in + lax.optimization_barrier(term_in.astype(jnp.bfloat16)).astype(jnp.float32)
            grad_out = grad_out + lax.optimization_barrier(term_out.astype(jnp.bfloat16)).astype(jnp.float32)
        return (back_part.reshape(groups, rows_per, width), gate_part.reshape(groups, rows_per),
                grad_in.astype(jnp.bfloat16), grad_out.astype(jnp.bfloat16))

    back_all, gate_all, w_in_grad, w_out_grad = lax.map(
        per_expert,
        (jnp.swapaxes(chosen, 0, 1), jnp.swapaxes(gates, 0, 1), jnp.swapaxes(x_slots, 0, 1), w_in, w_out))
    token_grad = jnp.zeros((groups, count.shape[1], width), jnp.float32)
    for group in range(groups):
        token_grad = token_grad.at[group, chosen[group].reshape(-1)].add(
            back_all[:, group].reshape(-1, width).astype(jnp.float32))
    return token_grad.astype(jnp.bfloat16), jnp.swapaxes(gate_all, 0, 1), w_in_grad, w_out_grad
```

```python
import jax
import jax.numpy as jnp
from jax import lax
from jax.sharding import PartitionSpec as P

SQRT_HALF = 0.7071067811865476
INV_ROOT_TWO_PI = 0.3989422804014327
PEER = 6
CHUNKS = 1
F32 = jnp.float32
BF16 = jnp.bfloat16


def dot(a, b, dims):
    return lax.dot_general(a, b, (dims, ((), ())), preferred_element_type=F32)


def shards(out_grad, count, chosen, gates, x_slots, w_in, w_out):
    tok_rows = out_grad.shape[1]
    width = out_grad.shape[2]
    experts = chosen.shape[1]
    cap = chosen.shape[2]
    slots = experts * cap
    hidden_share = w_in.shape[2]
    n = lax.axis_size("dp")
    owners = lax.axis_size("expert")
    me = lax.axis_index("dp")
    quarter = width // n
    per = n // CHUNKS
    wide = quarter // CHUNKS
    rows = n * PEER

    def shift(x, s):
        return lax.ppermute(x, "dp", [(a, (a + s) % n) for a in range(n)])

    def at(s):
        return lax.rem(me + (s + n), n)

    def columns(x, q):
        return lax.dynamic_slice_in_dim(x, q * quarter, quarter, axis=x.ndim - 1)

    def spread(block, shape, dtype, place):
        out = jnp.zeros(shape, dtype)
        out = lax.dynamic_update_slice(out, block(at(0)), place(at(0)))
        for s in range(1, n):
            out = lax.dynamic_update_slice(out, shift(block(at(s)), s), place(at(-s)))
        return out

    def gather_groups(x):
        out = jnp.zeros((n,) + x.shape, x.dtype)
        zeros = (0,) * x.ndim
        out = lax.dynamic_update_slice(out, x[None], (at(0),) + zeros)
        for s in range(1, n):
            out = lax.dynamic_update_slice(out, shift(x, s)[None], (at(-s),) + zeros)
        return out

    def gather_hidden(x):
        return jnp.concatenate([x] + [shift(x, s) for s in range(1, n)], axis=-1)

    def reduce_hidden(x):
        total = x[..., :hidden_share]
        for s in range(1, n):
            total = total + shift(x[..., s * hidden_share : (s + 1) * hidden_share], -s)
        return total

    source_ids = jnp.arange(owners, dtype=jnp.int32)
    slot_ids = jnp.arange(slots, dtype=jnp.int32)
    earlier = (slot_ids[None, :] < slot_ids[:, None]).astype(BF16)

    def places(tokens):
        source = lax.div(tokens, tok_rows)
        onehot = (source[:, None] == source_ids[None, :]).astype(BF16)
        before = dot(earlier, onehot, ((1,), (0,)))
        rank = jnp.sum(before * onehot.astype(F32), axis=1).astype(jnp.int32)
        return source, rank, onehot

    tokens = chosen.reshape(slots)
    _, rank, onehot = places(tokens)
    local_row = lax.rem(tokens, tok_rows)
    ranks = jnp.arange(8, dtype=jnp.int32)
    marked = jnp.where(rank[:, None] == ranks[None, :], (local_row + 1)[:, None], 0).astype(BF16)
    request = dot(onehot, marked, ((0,), (0,))).astype(jnp.int32) - 1
    request = jnp.broadcast_to(request[None], (n, owners, 8)).reshape(n * owners, 8)
    asked = lax.all_to_all(request, ("dp", "expert"), split_axis=0, concat_axis=0, tiled=True)
    asked = asked.reshape(n, owners, 8)[:, :, :PEER]

    table = out_grad[0]
    og = spread(lambda q: columns(table, q)[None], (n, tok_rows, quarter), BF16, lambda q: (q, 0, 0))

    inputs = x_slots.reshape(slots, width)
    xs = spread(lambda q: columns(inputs, q)[None], (n, slots, quarter), BF16, lambda q: (q, 0, 0))
    xs = xs.reshape(n, experts, cap, quarter)

    def w_in_block(q):
        return lax.dynamic_slice_in_dim(w_in, q * quarter, quarter, axis=1)

    w_in_all = jnp.concatenate(
        [w_in_block(at(0))] + [shift(w_in_block(at(s)), s) for s in range(1, n)], axis=2
    )
    w_out_all = jnp.concatenate(
        [columns(w_out, at(0))] + [shift(columns(w_out, at(s)), s) for s in range(1, n)], axis=1
    )

    counts = lax.all_gather(count[0], "expert", axis=0, tiled=True)
    slot_count = counts[tokens].astype(F32)
    scale = gather_groups(gates.reshape(slots) / slot_count).reshape(n, experts, cap, 1)
    tokens_all = gather_groups(tokens)

    pre = reduce_hidden(
        jnp.einsum("gecd,edf->gecf", xs, w_in_all, preferred_element_type=F32)
    )
    normal_cdf = 0.5 * (1.0 + lax.erf(pre * SQRT_HALF))
    slope = normal_cdf + pre * jnp.exp(-0.5 * pre * pre) * INV_ROOT_TWO_PI
    hidden_f = pre * normal_cdf
    hidden = hidden_f.astype(BF16).astype(F32)
    hidden_all = gather_hidden((scale * hidden_f).astype(BF16))
    slope = scale * slope

    part = jnp.arange(CHUNKS, dtype=jnp.int32)
    member = jnp.arange(per, dtype=jnp.int32)
    upstream = []
    pre_grads = []
    gate_parts = []
    sums = []
    for chunk in range(CHUNKS):
        low = chunk * per
        wanted = asked[low : low + per].transpose(1, 0, 2)[:, None]
        start = (part[:, None] * per + member[None, :])[None, :, :, None] * tok_rows
        pick = jnp.where(wanted >= 0, start + wanted, -1).reshape(owners * rows)
        pick = (pick[:, None] == jnp.arange(n * tok_rows, dtype=jnp.int32)[None, :]).astype(BF16)
        held = og[low : low + per].reshape(per * tok_rows, CHUNKS, wide)
        held = held.transpose(1, 0, 2).reshape(n * tok_rows, wide)
        sent = dot(pick, held, ((1,), (0,))).astype(BF16).reshape(owners, rows, wide)
        got = lax.all_to_all(sent, "expert", split_axis=0, concat_axis=0, tiled=True)
        got = got.reshape(owners * rows, wide)

        place = []
        for g in range(per):
            source, rank, _ = places(tokens_all[low + g])
            place.append(source * rows + g * PEER + rank)
        place = jnp.stack(place)[None] + (part * (per * PEER))[:, None, None]
        place = place.reshape(n * slots)
        place = (place[:, None] == jnp.arange(owners * rows, dtype=jnp.int32)[None, :]).astype(BF16)
        up = dot(place, got, ((1,), (0,))).astype(BF16)
        up = up.reshape(CHUNKS, per * slots, wide).transpose(1, 0, 2)
        up = up.reshape(per, experts, cap, quarter)
        upstream.append(up)
        project = reduce_hidden(
            jnp.einsum("gecd,efd->gecf", up, w_out_all, preferred_element_type=F32)
        )
        gate_parts.append(jnp.sum(hidden[low : low + per] * project, axis=3))
        pre_grad = gather_hidden((project * slope[low : low + per]).astype(BF16))
        pre_grads.append(pre_grad)
        back = jnp.einsum("gecf,edf->gecd", pre_grad, w_in_all, preferred_element_type=F32).astype(BF16)
        back = back.reshape(per * slots, CHUNKS, wide).transpose(1, 0, 2).reshape(n * slots, wide)
        outgoing = dot(place, back, ((0,), (0,))).astype(BF16).reshape(owners, rows, wide)
        returned = lax.all_to_all(outgoing, "expert", split_axis=0, concat_axis=0, tiled=True)
        total = dot(pick, returned.reshape(owners * rows, wide), ((0,), (0,))).astype(BF16)
        total = total.reshape(CHUNKS, per * tok_rows, wide).transpose(1, 0, 2)
        sums.append(total.reshape(per, tok_rows, quarter))

    upstream = jnp.concatenate(upstream)
    pre_grads = jnp.concatenate(pre_grads)
    gate_parts = jnp.concatenate(gate_parts).reshape(n, slots)
    sums = jnp.concatenate(sums)

    def group(x, q):
        return lax.dynamic_index_in_dim(x, q, axis=0, keepdims=False)

    gate_sum = group(gate_parts, at(0))
    for s in range(1, n):
        gate_sum = gate_sum + shift(group(gate_parts, at(s)), s)
    gate_grad = (gate_sum / slot_count).reshape(1, experts, cap)

    grad_in = jnp.einsum("gecd,gecf->edf", xs, pre_grads, preferred_element_type=F32).astype(BF16)
    grad_out = jnp.einsum("gecf,gecd->efd", hidden_all, upstream, preferred_element_type=F32).astype(BF16)

    def take(x, s, axis):
        return lax.slice_in_dim(x, s * hidden_share, (s + 1) * hidden_share, axis=axis)

    w_in_grad = jnp.zeros(w_in.shape, BF16)
    w_out_grad = jnp.zeros(w_out.shape, BF16)
    for s in range(n):
        block_in = take(grad_in, s, 2)
        block_out = take(grad_out, s, 1)
        if s:
            block_in = shift(block_in, -s)
            block_out = shift(block_out, -s)
        w_in_grad = lax.dynamic_update_slice(w_in_grad, block_in, (0, at(s) * quarter, 0))
        w_out_grad = lax.dynamic_update_slice(w_out_grad, block_out, (0, 0, at(s) * quarter))

    token_grad = spread(
        lambda q: group(sums, q), (tok_rows, width), BF16, lambda q: (0, q * quarter)
    )[None]
    return (token_grad, gate_grad, w_in_grad, w_out_grad)


def solution(mesh):
    return jax.shard_map(
        shards,
        mesh=mesh,
        in_specs=(
            P("dp", "expert", None),
            P("dp", "expert"),
            P("dp", "expert", None),
            P("dp", "expert", None),
            P("dp", "expert", None, None),
            P("expert", None, "dp"),
            P("expert", "dp", None),
        ),
        out_specs=(
            P("dp", "expert", None),
            P("dp", "expert", None),
            P("expert", None, "dp"),
            P("expert", "dp", None),
        ),
        check_vma=False,
    )
```

```python
import functools

import jax
import jax.numpy as jnp
from jax import lax
from jax.experimental import pallas as pl
from jax.experimental.pallas import tpu as pltpu
from jax.sharding import PartitionSpec as P

SQRT_HALF = 0.7071067811865476
INV_ROOT_TWO_PI = 0.3989422804014327
PEER = 6
F32 = jnp.float32
BF16 = jnp.bfloat16
VMEM_BYTES = 40 * 1024 * 1024


def dot(a, b, dims):
    return lax.dot_general(a, b, (dims, ((), ())), preferred_element_type=F32)


def whole(shape):
    return pl.BlockSpec(shape, lambda *_: (0,) * len(shape))


def call(kernel, outs, args, in_specs=None, out_specs=None, grid=(1,), scratch=(), flops=0, scalars=0):
    shapes = [jax.ShapeDtypeStruct(shape, dtype) for shape, dtype in outs]
    sizes = [a.size * a.dtype.itemsize for a in args]
    sizes += [s.size * s.dtype.itemsize for s in shapes]
    in_specs = in_specs or [whole(a.shape) for a in args[scalars:]]
    out_specs = out_specs or [whole(s.shape) for s in shapes]
    return pl.pallas_call(
        kernel,
        out_shape=shapes,
        grid_spec=pltpu.PrefetchScalarGridSpec(
            num_scalar_prefetch=scalars,
            grid=grid,
            in_specs=in_specs,
            out_specs=out_specs,
            scratch_shapes=list(scratch),
        ),
        compiler_params=pltpu.CompilerParams(vmem_limit_bytes=VMEM_BYTES),
        cost_estimate=pl.CostEstimate(flops=flops, bytes_accessed=sum(sizes), transcendentals=0),
    )(*args)


def pack_kernel(n, tok, pick, *refs):
    blocks, sent, held = refs[:n], refs[n], refs[n + 1]

    @pl.when(pl.program_id(0) == 0)
    def _():
        for p in range(n):
            held[p * tok : (p + 1) * tok] = blocks[p][...]

    ids = lax.broadcasted_iota(jnp.int32, (pick.shape[0], n * tok), 1)
    onehot = jnp.where(pick[...] == ids, 1.0, 0.0).astype(BF16)
    sent[...] = dot(onehot, held[...], ((1,), (0,))).astype(BF16)


def project_kernel(n, cap, into, got, *refs):
    ws, up, outs, wide = refs[:n], refs[n], refs[n + 1 : 2 * n + 1], refs[2 * n + 1]
    share = ws[0].shape[1]
    for s in range(n):
        wide[s * share : (s + 1) * share] = ws[s][0]
    ids = lax.broadcasted_iota(jnp.int32, (n * cap, got.shape[0]), 1)
    onehot = jnp.where(into[...] == ids, 1.0, 0.0).astype(BF16)
    up[...] = dot(onehot, got[...], ((1,), (0,))).astype(BF16)
    part = dot(up[...], wide[...], ((1,), (1,)))
    for s in range(n):
        for p in range(n):
            low = ((p - s) % n) * cap
            block = part[p * cap : (p + 1) * cap, s * share : (s + 1) * share]
            outs[s][low : low + cap] = block.astype(outs[s].dtype)


def back_kernel(n, cap, me, place, *refs):
    ps, ws, out = refs[:n], refs[n : 2 * n], refs[2 * n]
    wide, tall, back = refs[2 * n + 1 :]
    experts, width, share = ws[0].shape
    thin = width // n
    step = out.shape[1] // 2
    p = pl.program_id(0)

    @pl.when(p == 0)
    def _():
        for e in range(experts):
            for s in range(n):
                wide[:, s * share : (s + 1) * share] = ws[s][e]
                for g in range(n):
                    low = (e * n + (g - s) % n) * cap
                    tall[g * cap : (g + 1) * cap, s * share : (s + 1) * share] = ps[s][low : low + cap]
            mine = dot(tall[...], wide[...], ((1,), (1,))).astype(BF16)
            for g in range(n):
                back[g, e * cap : (e + 1) * cap] = mine[g * cap : (g + 1) * cap]

    where = place[pl.ds(p, 1)]
    for t in range(2):
        ids = lax.broadcasted_iota(jnp.int32, (step, experts * cap), 0) + t * step
        total = jnp.zeros((step, thin), F32)
        for b in range(n):
            onehot = jnp.where(ids == where + b * PEER, 1.0, 0.0).astype(BF16)
            total = total + dot(onehot, back[p, :, b * thin : (b + 1) * thin], ((1,), (0,)))
        out[0, t * step : (t + 1) * step] = total.astype(BF16)


def grad_out_kernel(n, cap, *refs):
    hs, up, outs, tall = refs[:n], refs[n], refs[n + 1 : 2 * n + 1], refs[2 * n + 1]
    experts, share, _ = outs[0].shape
    for s in range(n):
        for e in range(experts):
            for p in range(n):
                low = (e * n + (p - s) % n) * cap
                high = (e * n + p) * cap
                tall[high : high + cap, s * share : (s + 1) * share] = hs[s][low : low + cap]
    for e in range(experts):
        rows = slice(e * n * cap, (e + 1) * n * cap)
        grad = dot(tall[rows], up[rows], ((0,), (0,)))
        for s in range(n):
            outs[s][e] = grad[s * share : (s + 1) * share].astype(BF16)


def sum_kernel(n, tok, home, returned, out, onehot):
    rows, thin = returned.shape[1:]

    @pl.when(pl.program_id(0) == 0)
    def _():
        ids = lax.broadcasted_iota(jnp.int32, (n * tok, rows), 0)
        onehot[...] = jnp.where(home[...] == ids, 1.0, 0.0).astype(BF16)

    total = dot(onehot[...], returned[0], ((1,), (0,))).astype(BF16)
    for b in range(n):
        out[:, b * thin : (b + 1) * thin] = total[b * tok : (b + 1) * tok]


def shards(out_grad, count, chosen, gates, x_slots, w_in, w_out):
    tok = out_grad.shape[1]
    width = out_grad.shape[2]
    experts, cap = chosen.shape[1:]
    slots = experts * cap
    share = w_in.shape[2]
    n = lax.axis_size("dp")
    owners = lax.axis_size("expert")
    me = lax.axis_index("dp")
    quarter = width // n
    thin = quarter // n
    rows = n * PEER
    every = n * slots

    def shift(x, s):
        return lax.ppermute(x, "dp", [(a, (a + s) % n) for a in range(n)])

    def at(s):
        return lax.rem(me + (s + n), n)

    def columns(x, s):
        return lax.dynamic_slice_in_dim(x, at(s) * quarter, quarter, axis=x.ndim - 1)

    def forward(blocks):
        return [blocks[0]] + [shift(blocks[s], s) for s in range(1, n)]

    def backward(blocks):
        return [blocks[0]] + [shift(blocks[s], -s) for s in range(1, n)]

    def reduced(blocks):
        total = blocks[0]
        for block in backward(blocks)[1:]:
            total = total + block.astype(F32)
        return total

    inputs = lax.all_gather(x_slots.reshape(slots, width), "dp", axis=0, tiled=True)
    inputs = inputs.reshape(n, experts, cap, width)

    def turned(x):
        return [lax.dynamic_index_in_dim(x, at(-p), 0, keepdims=False) for p in range(n)]

    facts = jnp.stack([gates.reshape(slots), chosen.reshape(slots).astype(F32)])
    facts = jnp.stack(forward([facts] * n))
    tokens = facts[:, 1].astype(jnp.int32)
    source = lax.div(tokens, tok)
    onehot = (source[:, :, None] == jnp.arange(owners, dtype=jnp.int32)).astype(BF16)
    slot_ids = jnp.arange(slots, dtype=jnp.int32)
    earlier = (slot_ids[None, :] < slot_ids[:, None]).astype(BF16)
    before = jnp.einsum("st,ptk->psk", earlier, onehot, preferred_element_type=F32)
    rank = jnp.sum(before * onehot.astype(F32), axis=2).astype(jnp.int32)
    marked = rank[:, :, None] == jnp.arange(8, dtype=jnp.int32)
    marked = jnp.where(marked, (lax.rem(tokens, tok) + 1)[:, :, None], 0).astype(BF16)
    request = jnp.einsum("psk,psr->kpr", onehot, marked, preferred_element_type=F32)
    request = request.astype(jnp.int32).reshape(owners, n * 8) - 1
    asked = lax.all_to_all(request, "expert", split_axis=0, concat_axis=0, tiled=True)
    asked = asked.reshape(owners, n, 8)[:, :, :PEER]

    spread = jnp.maximum(count[0], 1).astype(F32)[:, None]
    table = (out_grad[0].astype(F32) / spread).astype(BF16)
    held = forward([columns(table, s) for s in range(n)])

    place = source * rows + rank
    scale = facts[:, 0].reshape(n, experts, cap).transpose(1, 0, 2).reshape(every, 1)
    into = place + jnp.arange(n, dtype=jnp.int32)[:, None] * PEER
    into = into.reshape(n, experts, cap).transpose(1, 0, 2).reshape(every, 1)

    own_out = [columns(w_out, s) for s in range(n)]
    own_in = [lax.dynamic_slice_in_dim(w_in, at(s) * quarter, quarter, axis=1) for s in range(n)]
    w_out_all = forward(own_out)
    w_in_all = forward(own_in)
    inputs, w_in_all = lax.optimization_barrier((inputs, w_in_all))

    start = jnp.arange(n, dtype=jnp.int32)[None, :, None] * tok
    pick = jnp.where(asked >= 0, asked + start, -1).reshape(owners * rows, 1)
    (sent,) = call(
        functools.partial(pack_kernel, n, tok),
        [((owners * rows, quarter), BF16)],
        [pick, *held],
        [pl.BlockSpec((owners * rows // 6, 1), lambda t: (t, 0))] + [whole((tok, quarter))] * n,
        [pl.BlockSpec((owners * rows // 6, quarter), lambda t: (t, 0))],
        (6,),
        [pltpu.VMEM((n * tok, quarter), BF16)],
        flops=2 * owners * rows * n * tok * quarter,
    )
    got = lax.all_to_all(
        sent.reshape(owners, rows, quarter), "expert", split_axis=0, concat_axis=0, tiled=True
    )

    pre = jnp.einsum("gecd,edf->gecf", inputs, w_in, preferred_element_type=F32)
    pre = jnp.stack(turned(pre), 1).reshape(every, share)
    normal_cdf = 0.5 * (1.0 + lax.erf(pre * SQRT_HALF))
    slope = scale * (normal_cdf + pre * jnp.exp(-0.5 * pre * pre) * INV_ROOT_TWO_PI)
    hidden = pre * normal_cdf
    hidden_all = forward([(scale * hidden).astype(BF16)] * n)
    hidden = hidden.astype(BF16)

    partials = [((every, share), F32)] + [((every, share), BF16)] * (n - 1)
    up, *partial = call(
        functools.partial(project_kernel, n, cap),
        [((every, quarter), BF16)] + partials,
        [into, got.reshape(owners * rows, quarter), *w_out_all],
        [pl.BlockSpec((n * cap, 1), lambda e: (e, 0)), whole((owners * rows, quarter))]
        + [pl.BlockSpec((1, share, quarter), lambda e: (e, 0, 0))] * n,
        [pl.BlockSpec((n * cap, quarter), lambda e: (e, 0))]
        + [pl.BlockSpec((n * cap, share), lambda e: (e, 0))] * n,
        (experts,),
        [pltpu.VMEM((n * share, quarter), BF16)],
        flops=2 * every * quarter * (n * share + owners * rows),
    )
    project = reduced(partial)
    project, hidden_all = lax.optimization_barrier((project, hidden_all))
    gate = jnp.sum(hidden.astype(F32) * project, axis=1).reshape(experts, n, cap)
    gate = reduced([gate[:, p] for p in range(n)])
    pre_grad = forward([(project * slope).astype(BF16)] * n)
    pre_grad, gate = lax.optimization_barrier((pre_grad, gate))
    gate_grad = gate.reshape(1, experts, cap)

    out_blocks = call(
        functools.partial(grad_out_kernel, n, cap),
        [((experts, share, quarter), BF16)] * n,
        [*hidden_all, up],
        scratch=[pltpu.VMEM((every, n * share), BF16)],
        flops=2 * every * quarter * n * share,
    )
    pre_grad, out_blocks = lax.optimization_barrier((pre_grad, out_blocks))
    out_blocks = backward(out_blocks)

    (outgoing,) = call(
        functools.partial(back_kernel, n, cap),
        [((n, owners * rows, thin), BF16)],
        [me.reshape(1), place, *pre_grad, *w_in_all],
        out_specs=[
            pl.BlockSpec((1, owners * rows, thin), lambda p, m: (lax.rem(m[0] + n - p, n), 0, 0))
        ],
        grid=(n,),
        scratch=[
            pltpu.VMEM((quarter, n * share), BF16),
            pltpu.VMEM((n * cap, n * share), BF16),
            pltpu.VMEM((n, slots, quarter), BF16),
        ],
        flops=2 * every * quarter * (n * share + owners * rows),
        scalars=1,
    )
    returned = lax.all_to_all(
        outgoing.reshape(n * owners, rows, thin),
        ("dp", "expert"),
        split_axis=0,
        concat_axis=0,
        tiled=True,
    )

    own_grad = pre_grad[0].reshape(experts, n, cap, share).transpose(1, 0, 2, 3)
    own_grad = jnp.stack(turned(own_grad))
    w_in_grad = jnp.einsum("gecd,gecf->edf", inputs, own_grad, preferred_element_type=F32).astype(BF16)
    w_out_grad = jnp.zeros(w_out.shape, BF16)
    for s in range(n):
        w_out_grad = lax.dynamic_update_slice(w_out_grad, out_blocks[s], (0, 0, at(s) * quarter))

    mine = asked[:, :1]
    home = jnp.where(mine >= 0, mine + jnp.arange(n, dtype=jnp.int32)[None, :, None] * tok, -1)
    (token_grad,) = call(
        functools.partial(sum_kernel, n, tok),
        [((tok, width), BF16)],
        [home.reshape(1, owners * rows), returned.reshape(n, owners * rows, thin)],
        [whole((1, owners * rows)), pl.BlockSpec((1, owners * rows, thin), lambda q: (q, 0, 0))],
        [pl.BlockSpec((tok, quarter), lambda q: (0, q))],
        (n,),
        [pltpu.VMEM((n * tok, owners * rows), BF16)],
        flops=2 * n * tok * owners * rows * quarter,
    )
    return (token_grad[None], gate_grad, w_in_grad, w_out_grad)


def solution(mesh):
    return jax.shard_map(
        shards,
        mesh=mesh,
        in_specs=(
            P("dp", "expert", None),
            P("dp", "expert"),
            P("dp", "expert", None),
            P("dp", "expert", None),
            P("dp", "expert", None, None),
            P("expert", None, "dp"),
            P("expert", "dp", None),
        ),
        out_specs=(
            P("dp", "expert", None),
            P("dp", "expert", None),
            P("expert", None, "dp"),
            P("expert", "dp", None),
        ),
        check_vma=False,
    )
```

```python
import functools

import jax
import jax.numpy as jnp
from jax import lax
from jax.experimental import pallas as pl
from jax.experimental.pallas import tpu as pltpu
from jax.sharding import PartitionSpec as P

SQRT_HALF = 0.7071067811865476
INV_ROOT_TWO_PI = 0.3989422804014327
PEER = 6
F32 = jnp.float32
BF16 = jnp.bfloat16
VMEM_BYTES = 40 * 1024 * 1024


def dot(a, b, dims):
    return lax.dot_general(a, b, (dims, ((), ())), preferred_element_type=F32)


def whole(shape):
    return pl.BlockSpec(shape, lambda *_: (0,) * len(shape))


def call(kernel, outs, args, in_specs=None, out_specs=None, grid=(1,), scratch=(), flops=0, scalars=0):
    shapes = [jax.ShapeDtypeStruct(shape, dtype) for shape, dtype in outs]
    sizes = [a.size * a.dtype.itemsize for a in args]
    sizes += [s.size * s.dtype.itemsize for s in shapes]
    in_specs = in_specs or [whole(a.shape) for a in args[scalars:]]
    out_specs = out_specs or [whole(s.shape) for s in shapes]
    return pl.pallas_call(
        kernel,
        out_shape=shapes,
        grid_spec=pltpu.PrefetchScalarGridSpec(
            num_scalar_prefetch=scalars,
            grid=grid,
            in_specs=in_specs,
            out_specs=out_specs,
            scratch_shapes=list(scratch),
        ),
        compiler_params=pltpu.CompilerParams(vmem_limit_bytes=VMEM_BYTES),
        cost_estimate=pl.CostEstimate(flops=flops, bytes_accessed=sum(sizes), transcendentals=0),
    )(*args)


def column(rows):
    size = rows.shape[1]
    eye = lax.broadcasted_iota(jnp.int32, (size, size), 0) == lax.broadcasted_iota(jnp.int32, (size, size), 1)
    parts = [
        jnp.sum(jnp.where(eye, rows[k : k + 1], 0), axis=1, keepdims=True) for k in range(rows.shape[0])
    ]
    return jnp.concatenate(parts, axis=0)


def pack_kernel(n, tok, pick, *refs):
    blocks, sent, held = refs[:n], refs[n], refs[n + 1]

    @pl.when(pl.program_id(0) == 0)
    def _():
        for p in range(n):
            held[p * tok : (p + 1) * tok] = blocks[p][...]

    ids = lax.broadcasted_iota(jnp.int32, (pick.shape[0], n * tok), 1)
    onehot = jnp.where(pick[...] == ids, 1.0, 0.0).astype(BF16)
    sent[...] = dot(onehot, held[...], ((1,), (0,))).astype(BF16)


def project_kernel(n, cap, into, got, *refs):
    ws, up, outs, wide = refs[:n], refs[n], refs[n + 1 : 2 * n + 1], refs[2 * n + 1]
    share = ws[0].shape[1]
    for s in range(n):
        wide[s * share : (s + 1) * share] = ws[s][0]
    ids = lax.broadcasted_iota(jnp.int32, (n * cap, got.shape[0]), 1)
    onehot = jnp.where(column(into[0]) == ids, 1.0, 0.0).astype(BF16)
    up[...] = dot(onehot, got[...], ((1,), (0,))).astype(BF16)
    part = dot(up[...], wide[...], ((1,), (1,)))
    for s in range(n):
        for p in range(n):
            low = ((p - s) % n) * cap
            block = part[p * cap : (p + 1) * cap, s * share : (s + 1) * share]
            outs[s][low : low + cap] = block.astype(outs[s].dtype)


def back_kernel(n, cap, me, place, *refs):
    ps, ws, out = refs[:n], refs[n : 2 * n], refs[2 * n]
    wide, tall, back = refs[2 * n + 1 :]
    experts, width, share = ws[0].shape
    thin = width // n
    step = out.shape[1] // 2
    p = pl.program_id(0)

    @pl.when(p == 0)
    def _():
        for e in range(experts):
            for s in range(n):
                wide[:, s * share : (s + 1) * share] = ws[s][e]
                for g in range(n):
                    low = (e * n + (g - s) % n) * cap
                    tall[g * cap : (g + 1) * cap, s * share : (s + 1) * share] = ps[s][low : low + cap]
            mine = dot(tall[...], wide[...], ((1,), (1,))).astype(BF16)
            for g in range(n):
                back[g, e * cap : (e + 1) * cap] = mine[g * cap : (g + 1) * cap]

    owners = out.shape[1] // (n * PEER)
    ids = lax.broadcasted_iota(jnp.int32, (owners * 8, experts * cap), 0)
    onehot = jnp.where(ids == place[pl.ds(p, 1)], 1.0, 0.0).astype(BF16)
    full = dot(onehot, back[p], ((1,), (0,))).reshape(owners, 8, width)
    row = lax.broadcasted_iota(jnp.int32, (owners, 8, thin), 1)
    first = full[:, :, :thin]
    second = pltpu.roll(full[:, :, thin : 2 * thin], 6, 1)
    third = pltpu.roll(full[:, :, 2 * thin : 3 * thin], 4, 1)
    fourth = pltpu.roll(full[:, :, 3 * thin :], 2, 1)
    tiles = [
        jnp.where(row < 6, first, second),
        jnp.where(row < 4, second, third),
        jnp.where(row < 2, third, fourth),
    ]
    out[0] = jnp.concatenate(tiles, axis=1).reshape(owners * n * PEER, thin).astype(BF16)


def grad_out_kernel(n, cap, *refs):
    hs, up, outs, tall = refs[:n], refs[n], refs[n + 1 : 2 * n + 1], refs[2 * n + 1]
    experts, share, _ = outs[0].shape
    for s in range(n):
        for e in range(experts):
            for p in range(n):
                low = (e * n + (p - s) % n) * cap
                high = (e * n + p) * cap
                tall[high : high + cap, s * share : (s + 1) * share] = hs[s][low : low + cap]
    for e in range(experts):
        rows = slice(e * n * cap, (e + 1) * n * cap)
        grad = dot(tall[rows], up[rows], ((0,), (0,)))
        for s in range(n):
            outs[s][e] = grad[s * share : (s + 1) * share].astype(BF16)


def sum_kernel(n, tok, home, returned, out, onehot):
    rows, thin = returned.shape[1:]

    @pl.when(pl.program_id(0) == 0)
    def _():
        ids = lax.broadcasted_iota(jnp.int32, (n * tok, rows), 0)
        onehot[...] = jnp.where(home[...] == ids, 1.0, 0.0).astype(BF16)

    total = dot(onehot[...], returned[0], ((1,), (0,))).astype(BF16)
    for b in range(n):
        out[:, b * thin : (b + 1) * thin] = total[b * tok : (b + 1) * tok]


def shards(out_grad, count, chosen, gates, x_slots, w_in, w_out):
    tok = out_grad.shape[1]
    width = out_grad.shape[2]
    experts, cap = chosen.shape[1:]
    slots = experts * cap
    share = w_in.shape[2]
    n = lax.axis_size("dp")
    owners = lax.axis_size("expert")
    me = lax.axis_index("dp")
    quarter = width // n
    thin = quarter // n
    rows = n * PEER
    every = n * slots

    def shift(x, s):
        return lax.ppermute(x, "dp", [(a, (a + s) % n) for a in range(n)])

    def at(s):
        return lax.rem(me + (s + n), n)

    def columns(x, s):
        return lax.dynamic_slice_in_dim(x, at(s) * quarter, quarter, axis=x.ndim - 1)

    def forward(blocks):
        return [blocks[0]] + [shift(blocks[s], s) for s in range(1, n)]

    def backward(blocks):
        return [blocks[0]] + [shift(blocks[s], -s) for s in range(1, n)]

    def reduced(blocks):
        total = blocks[0]
        for block in backward(blocks)[1:]:
            total = total + block.astype(F32)
        return total

    inputs = lax.all_gather(x_slots.reshape(slots, width), "dp", axis=0, tiled=True)
    inputs = inputs.reshape(n, experts, cap, width)

    def turned(x):
        return [lax.dynamic_index_in_dim(x, at(-p), 0, keepdims=False) for p in range(n)]

    facts = jnp.stack([gates.reshape(slots), chosen.reshape(slots).astype(F32)])
    facts = jnp.stack(forward([facts] * n))
    tokens = facts[:, 1].astype(jnp.int32)
    source = lax.div(tokens, tok)
    onehot = (source[:, :, None] == jnp.arange(owners, dtype=jnp.int32)).astype(BF16)
    slot_ids = jnp.arange(slots, dtype=jnp.int32)
    earlier = (slot_ids[None, :] < slot_ids[:, None]).astype(BF16)
    before = jnp.einsum("st,ptk->psk", earlier, onehot, preferred_element_type=F32)
    rank = jnp.sum(before * onehot.astype(F32), axis=2).astype(jnp.int32)
    marked = rank[:, :, None] == jnp.arange(8, dtype=jnp.int32)
    marked = jnp.where(marked, (lax.rem(tokens, tok) + 1)[:, :, None], 0).astype(BF16)
    request = jnp.einsum("psk,psr->kpr", onehot, marked, preferred_element_type=F32)
    request = request.astype(jnp.int32).reshape(owners, n * 8) - 1
    asked = lax.all_to_all(request, "expert", split_axis=0, concat_axis=0, tiled=True)
    asked = asked.reshape(owners, n, 8)[:, :, :PEER]

    spread = jnp.maximum(count[0], 1).astype(F32)[:, None]
    table = (out_grad[0].astype(F32) / spread).astype(BF16)
    held = forward([columns(table, s) for s in range(n)])

    place = source * rows + rank
    scale = facts[:, 0].reshape(n, experts, cap).transpose(1, 0, 2).reshape(every, 1)
    into = place + jnp.arange(n, dtype=jnp.int32)[:, None] * PEER
    into = into.reshape(n, experts, cap).transpose(1, 0, 2)

    own_out = [columns(w_out, s) for s in range(n)]
    own_in = [lax.dynamic_slice_in_dim(w_in, at(s) * quarter, quarter, axis=1) for s in range(n)]
    w_out_all = forward(own_out)
    own_in, w_out_all = lax.optimization_barrier((own_in, w_out_all))
    w_in_all = forward(own_in)
    inputs, w_in_all = lax.optimization_barrier((inputs, w_in_all))

    start = jnp.arange(n, dtype=jnp.int32)[None, :, None] * tok
    pick = jnp.where(asked >= 0, asked + start, -1).reshape(owners * rows, 1)
    (sent,) = call(
        functools.partial(pack_kernel, n, tok),
        [((owners * rows, quarter), BF16)],
        [pick, *held],
        [pl.BlockSpec((owners * rows // 6, 1), lambda t: (t, 0))] + [whole((tok, quarter))] * n,
        [pl.BlockSpec((owners * rows // 6, quarter), lambda t: (t, 0))],
        (6,),
        [pltpu.VMEM((n * tok, quarter), BF16)],
        flops=2 * owners * rows * n * tok * quarter,
    )
    got = lax.all_to_all(
        sent.reshape(owners, rows, quarter), "expert", split_axis=0, concat_axis=0, tiled=True
    )

    pre = jnp.einsum("gecd,edf->gecf", inputs, w_in, preferred_element_type=F32)
    pre = jnp.stack(turned(pre), 1).reshape(every, share)
    normal_cdf = 0.5 * (1.0 + lax.erf(pre * SQRT_HALF))
    slope = scale * (normal_cdf + pre * jnp.exp(-0.5 * pre * pre) * INV_ROOT_TWO_PI)
    hidden = pre * normal_cdf
    scaled = (scale * hidden).astype(BF16)
    hidden = hidden.astype(BF16)

    partials = [((every, share), F32)] + [((every, share), BF16)] * (n - 1)
    up, *partial = call(
        functools.partial(project_kernel, n, cap),
        [((every, quarter), BF16)] + partials,
        [into, got.reshape(owners * rows, quarter), *w_out_all],
        [pl.BlockSpec((1, n, cap), lambda e: (e, 0, 0)), whole((owners * rows, quarter))]
        + [pl.BlockSpec((1, share, quarter), lambda e: (e, 0, 0))] * n,
        [pl.BlockSpec((n * cap, quarter), lambda e: (e, 0))]
        + [pl.BlockSpec((n * cap, share), lambda e: (e, 0))] * n,
        (experts,),
        [pltpu.VMEM((n * share, quarter), BF16)],
        flops=2 * every * quarter * (n * share + owners * rows),
    )
    project = reduced(partial)
    gate = jnp.sum(hidden.astype(F32) * project, axis=1).reshape(experts, n, cap)
    pre_grad = forward([(project * slope).astype(BF16)] * n)

    (outgoing,) = call(
        functools.partial(back_kernel, n, cap),
        [((n, owners * rows, thin), BF16)],
        [me.reshape(1), source * 8 + rank, *pre_grad, *w_in_all],
        out_specs=[
            pl.BlockSpec((1, owners * rows, thin), lambda p, m: (lax.rem(m[0] + n - p, n), 0, 0))
        ],
        grid=(n,),
        scratch=[
            pltpu.VMEM((quarter, n * share), BF16),
            pltpu.VMEM((n * cap, n * share), BF16),
            pltpu.VMEM((n, slots, quarter), BF16),
        ],
        flops=2 * every * quarter * (n * share + owners * rows),
        scalars=1,
    )
    returned = lax.all_to_all(
        outgoing.reshape(n * owners, rows, thin),
        ("dp", "expert"),
        split_axis=0,
        concat_axis=0,
        tiled=True,
    )

    scaled, gate, pre_grad = lax.optimization_barrier((scaled, gate, pre_grad))
    hidden_all = forward([scaled] * n)
    gate = reduced([gate[:, p] for p in range(n)])
    hidden_all, gate = lax.optimization_barrier((hidden_all, gate))
    gate_grad = gate.reshape(1, experts, cap)
    out_blocks = call(
        functools.partial(grad_out_kernel, n, cap),
        [((experts, share, quarter), BF16)] * n,
        [*hidden_all, up],
        scratch=[pltpu.VMEM((every, n * share), BF16)],
        flops=2 * every * quarter * n * share,
    )
    out_blocks = backward(out_blocks)

    own_grad = pre_grad[0].reshape(experts, n, cap, share).transpose(1, 0, 2, 3)
    own_grad = jnp.stack(turned(own_grad))
    w_in_grad = jnp.einsum("gecd,gecf->edf", inputs, own_grad, preferred_element_type=F32).astype(BF16)
    w_out_grad = jnp.zeros(w_out.shape, BF16)
    for s in range(n):
        w_out_grad = lax.dynamic_update_slice(w_out_grad, out_blocks[s], (0, 0, at(s) * quarter))

    mine = asked[:, :1]
    home = jnp.where(mine >= 0, mine + jnp.arange(n, dtype=jnp.int32)[None, :, None] * tok, -1)
    (token_grad,) = call(
        functools.partial(sum_kernel, n, tok),
        [((tok, width), BF16)],
        [home.reshape(1, owners * rows), returned.reshape(n, owners * rows, thin)],
        [whole((1, owners * rows)), pl.BlockSpec((1, owners * rows, thin), lambda q: (q, 0, 0))],
        [pl.BlockSpec((tok, quarter), lambda q: (0, q))],
        (n,),
        [pltpu.VMEM((n * tok, owners * rows), BF16)],
        flops=2 * n * tok * owners * rows * quarter,
    )
    return (token_grad[None], gate_grad, w_in_grad, w_out_grad)


def solution(mesh):
    return jax.shard_map(
        shards,
        mesh=mesh,
        in_specs=(
            P("dp", "expert", None),
            P("dp", "expert"),
            P("dp", "expert", None),
            P("dp", "expert", None),
            P("dp", "expert", None, None),
            P("expert", None, "dp"),
            P("expert", "dp", None),
        ),
        out_specs=(
            P("dp", "expert", None),
            P("dp", "expert", None),
            P("expert", None, "dp"),
            P("expert", "dp", None),
        ),
        check_vma=False,
    )
```

```python
import functools

import jax
import jax.numpy as jnp
from jax import lax
from jax.experimental import pallas as pl
from jax.experimental.pallas import tpu as pltpu
from jax.sharding import PartitionSpec as P

SQRT_HALF = 0.7071067811865476
INV_ROOT_TWO_PI = 0.3989422804014327
PEER = 6
F32 = jnp.float32
BF16 = jnp.bfloat16
VMEM_BYTES = 28 * 1024 * 1024


def dot(a, b, dims):
    return lax.dot_general(a, b, (dims, ((), ())), preferred_element_type=F32)


def whole(shape):
    return pl.BlockSpec(shape, lambda *_: (0,) * len(shape))


def call(kernel, outs, args, in_specs=None, out_specs=None, grid=(1,), scratch=(), flops=0, scalars=0):
    shapes = [jax.ShapeDtypeStruct(shape, dtype) for shape, dtype in outs]
    sizes = [a.size * a.dtype.itemsize for a in args]
    sizes += [s.size * s.dtype.itemsize for s in shapes]
    in_specs = in_specs or [whole(a.shape) for a in args[scalars:]]
    out_specs = out_specs or [whole(s.shape) for s in shapes]
    return pl.pallas_call(
        kernel,
        out_shape=shapes,
        grid_spec=pltpu.PrefetchScalarGridSpec(
            num_scalar_prefetch=scalars,
            grid=grid,
            in_specs=in_specs,
            out_specs=out_specs,
            scratch_shapes=list(scratch),
        ),
        compiler_params=pltpu.CompilerParams(vmem_limit_bytes=VMEM_BYTES),
        cost_estimate=pl.CostEstimate(flops=flops, bytes_accessed=sum(sizes), transcendentals=0),
    )(*args)


def column(rows):
    size = rows.shape[1]
    eye = lax.broadcasted_iota(jnp.int32, (size, size), 0) == lax.broadcasted_iota(jnp.int32, (size, size), 1)
    parts = [
        jnp.sum(jnp.where(eye, rows[k : k + 1], 0), axis=1, keepdims=True) for k in range(rows.shape[0])
    ]
    return jnp.concatenate(parts, axis=0)


def pack_kernel(n, tok, pick, *refs):
    blocks, sent, held = refs[:n], refs[n], refs[n + 1]

    @pl.when(pl.program_id(0) == 0)
    def _():
        for p in range(n):
            held[p * tok : (p + 1) * tok] = blocks[p][...]

    ids = lax.broadcasted_iota(jnp.int32, (pick.shape[0], n * tok), 1)
    onehot = jnp.where(pick[...] == ids, 1.0, 0.0).astype(BF16)
    sent[...] = dot(onehot, held[...], ((1,), (0,))).astype(BF16)


def project_kernel(n, cap, into, got, wide, up, *outs):
    share = wide.shape[1] // n
    ids = lax.broadcasted_iota(jnp.int32, (n * cap, got.shape[0]), 1)
    onehot = jnp.where(column(into[0]) == ids, 1.0, 0.0).astype(BF16)
    up[...] = dot(onehot, got[...], ((1,), (0,))).astype(BF16)
    part = dot(up[...], wide[0], ((1,), (1,)))
    for s in range(n):
        for p in range(n):
            low = ((p - s) % n) * cap
            block = part[p * cap : (p + 1) * cap, s * share : (s + 1) * share]
            outs[s][low : low + cap] = block.astype(outs[s].dtype)


def back_kernel(n, cap, me, place, *refs):
    ps, wide, out, tall, back = refs[:n], *refs[n:]
    experts, width, _ = wide.shape
    share = wide.shape[2] // n
    thin = width // n
    step = out.shape[1] // 2
    p = pl.program_id(0)

    @pl.when(p == 0)
    def _():
        for e in range(experts):
            for s in range(n):
                for g in range(n):
                    low = (e * n + (g - s) % n) * cap
                    tall[g * cap : (g + 1) * cap, s * share : (s + 1) * share] = ps[s][low : low + cap]
            mine = dot(tall[...], wide[e], ((1,), (1,))).astype(BF16)
            for g in range(n):
                back[g, e * cap : (e + 1) * cap] = mine[g * cap : (g + 1) * cap]

    owners = out.shape[1] // (n * PEER)
    ids = lax.broadcasted_iota(jnp.int32, (owners * 8, experts * cap), 0)
    onehot = jnp.where(ids == place[pl.ds(p, 1)], 1.0, 0.0).astype(BF16)
    full = dot(onehot, back[p], ((1,), (0,))).reshape(owners, 8, width)
    row = lax.broadcasted_iota(jnp.int32, (owners, 8, thin), 1)
    first = full[:, :, :thin]
    second = pltpu.roll(full[:, :, thin : 2 * thin], 6, 1)
    third = pltpu.roll(full[:, :, 2 * thin : 3 * thin], 4, 1)
    fourth = pltpu.roll(full[:, :, 3 * thin :], 2, 1)
    tiles = [
        jnp.where(row < 6, first, second),
        jnp.where(row < 4, second, third),
        jnp.where(row < 2, third, fourth),
    ]
    out[0] = jnp.concatenate(tiles, axis=1).reshape(owners * n * PEER, thin).astype(BF16)


def grad_out_kernel(n, cap, *refs):
    hs, up, outs, tall = refs[:n], refs[n], refs[n + 1 : 2 * n + 1], refs[2 * n + 1]
    experts, share, _ = outs[0].shape
    for s in range(n):
        for e in range(experts):
            for p in range(n):
                low = (e * n + (p - s) % n) * cap
                high = (e * n + p) * cap
                tall[high : high + cap, s * share : (s + 1) * share] = hs[s][low : low + cap]
    for e in range(experts):
        rows = slice(e * n * cap, (e + 1) * n * cap)
        grad = dot(tall[rows], up[rows], ((0,), (0,)))
        for s in range(n):
            outs[s][e] = grad[s * share : (s + 1) * share].astype(BF16)


def sum_kernel(n, tok, home, returned, out, onehot):
    rows, thin = returned.shape[1:]

    @pl.when(pl.program_id(0) == 0)
    def _():
        ids = lax.broadcasted_iota(jnp.int32, (n * tok, rows), 0)
        onehot[...] = jnp.where(home[...] == ids, 1.0, 0.0).astype(BF16)

    total = dot(onehot[...], returned[0], ((1,), (0,))).astype(BF16)
    for b in range(n):
        out[:, b * thin : (b + 1) * thin] = total[b * tok : (b + 1) * tok]


def shards(out_grad, count, chosen, gates, x_slots, w_in, w_out):
    tok = out_grad.shape[1]
    width = out_grad.shape[2]
    experts, cap = chosen.shape[1:]
    slots = experts * cap
    share = w_in.shape[2]
    n = lax.axis_size("dp")
    owners = lax.axis_size("expert")
    me = lax.axis_index("dp")
    quarter = width // n
    thin = quarter // n
    rows = n * PEER
    every = n * slots

    def shift(x, s):
        return lax.ppermute(x, "dp", [(a, (a + s) % n) for a in range(n)])

    def at(s):
        return lax.rem(me + (s + n), n)

    def columns(x, s):
        return lax.dynamic_slice_in_dim(x, at(s) * quarter, quarter, axis=x.ndim - 1)

    def forward(blocks):
        return [blocks[0]] + [shift(blocks[s], s) for s in range(1, n)]

    def backward(blocks):
        return [blocks[0]] + [shift(blocks[s], -s) for s in range(1, n)]

    def reduced(blocks):
        total = blocks[0]
        for block in backward(blocks)[1:]:
            total = total + block.astype(F32)
        return total

    inputs = lax.all_gather(x_slots.reshape(slots, width), "dp", axis=0, tiled=True)
    inputs = inputs.reshape(n, experts, cap, width)

    def turned(x):
        return [lax.dynamic_index_in_dim(x, at(-p), 0, keepdims=False) for p in range(n)]

    facts = jnp.stack([gates.reshape(slots), chosen.reshape(slots).astype(F32)])
    facts = jnp.stack(forward([facts] * n))
    tokens = facts[:, 1].astype(jnp.int32)
    source = lax.div(tokens, tok)
    onehot = (source[:, :, None] == jnp.arange(owners, dtype=jnp.int32)).astype(BF16)
    slot_ids = jnp.arange(slots, dtype=jnp.int32)
    earlier = (slot_ids[None, :] < slot_ids[:, None]).astype(BF16)
    before = jnp.einsum("st,ptk->psk", earlier, onehot, preferred_element_type=F32)
    rank = jnp.sum(before * onehot.astype(F32), axis=2).astype(jnp.int32)
    marked = rank[:, :, None] == jnp.arange(8, dtype=jnp.int32)
    marked = jnp.where(marked, (lax.rem(tokens, tok) + 1)[:, :, None], 0).astype(BF16)
    request = jnp.einsum("psk,psr->kpr", onehot, marked, preferred_element_type=F32)
    request = request.astype(jnp.int32).reshape(owners, n * 8) - 1
    asked = lax.all_to_all(request, "expert", split_axis=0, concat_axis=0, tiled=True)
    asked = asked.reshape(owners, n, 8)[:, :, :PEER]

    spread = jnp.maximum(count[0], 1).astype(F32)[:, None]
    table = (out_grad[0].astype(F32) / spread).astype(BF16)
    held = forward([columns(table, s) for s in range(n)])

    place = source * rows + rank
    scale = facts[:, 0].reshape(n, experts, cap).transpose(1, 0, 2).reshape(every, 1)
    into = place + jnp.arange(n, dtype=jnp.int32)[:, None] * PEER
    into = into.reshape(n, experts, cap).transpose(1, 0, 2)

    own_out = [columns(w_out, s) for s in range(n)]
    own_in = [lax.dynamic_slice_in_dim(w_in, at(s) * quarter, quarter, axis=1) for s in range(n)]
    w_out_all = forward(own_out)
    own_in, w_out_all = lax.optimization_barrier((own_in, w_out_all))
    w_in_all = forward(own_in)
    w_out_wide = jnp.concatenate(w_out_all, axis=1)
    inputs, w_in_all = lax.optimization_barrier((inputs, w_in_all))

    start = jnp.arange(n, dtype=jnp.int32)[None, :, None] * tok
    pick = jnp.where(asked >= 0, asked + start, -1).reshape(owners * rows, 1)
    (sent,) = call(
        functools.partial(pack_kernel, n, tok),
        [((owners * rows, quarter), BF16)],
        [pick, *held],
        [pl.BlockSpec((owners * rows // 6, 1), lambda t: (t, 0))] + [whole((tok, quarter))] * n,
        [pl.BlockSpec((owners * rows // 6, quarter), lambda t: (t, 0))],
        (6,),
        [pltpu.VMEM((n * tok, quarter), BF16)],
        flops=2 * owners * rows * n * tok * quarter,
    )
    got = lax.all_to_all(
        sent.reshape(owners, rows, quarter), "expert", split_axis=0, concat_axis=0, tiled=True
    )

    pre = jnp.einsum("gecd,edf->gecf", inputs, w_in, preferred_element_type=F32)
    pre, w_in_all = lax.optimization_barrier((pre, w_in_all))
    w_in_wide = jnp.concatenate(w_in_all, axis=2)
    pre = jnp.stack(turned(pre), 1).reshape(every, share)
    normal_cdf = 0.5 * (1.0 + lax.erf(pre * SQRT_HALF))
    slope = scale * (normal_cdf + pre * jnp.exp(-0.5 * pre * pre) * INV_ROOT_TWO_PI)
    hidden = pre * normal_cdf
    scaled = (scale * hidden).astype(BF16)
    hidden = hidden.astype(BF16)

    partials = [((every, share), F32)] + [((every, share), BF16)] * (n - 1)
    up, *partial = call(
        functools.partial(project_kernel, n, cap),
        [((every, quarter), BF16)] + partials,
        [into, got.reshape(owners * rows, quarter), w_out_wide],
        [pl.BlockSpec((1, n, cap), lambda e: (e, 0, 0)), whole((owners * rows, quarter))]
        + [pl.BlockSpec((1, n * share, quarter), lambda e: (e, 0, 0))],
        [pl.BlockSpec((n * cap, quarter), lambda e: (e, 0))]
        + [pl.BlockSpec((n * cap, share), lambda e: (e, 0))] * n,
        (experts,),
        flops=2 * every * quarter * (n * share + owners * rows),
    )
    project = reduced(partial)
    gate = jnp.sum(hidden.astype(F32) * project, axis=1).reshape(experts, n, cap)
    pre_grad = forward([(project * slope).astype(BF16)] * n)

    (outgoing,) = call(
        functools.partial(back_kernel, n, cap),
        [((n, owners * rows, thin), BF16)],
        [me.reshape(1), source * 8 + rank, *pre_grad, w_in_wide],
        out_specs=[
            pl.BlockSpec((1, owners * rows, thin), lambda p, m: (lax.rem(m[0] + n - p, n), 0, 0))
        ],
        grid=(n,),
        scratch=[
            pltpu.VMEM((n * cap, n * share), BF16),
            pltpu.VMEM((n, slots, quarter), BF16),
        ],
        flops=2 * every * quarter * (n * share + owners * rows),
        scalars=1,
    )
    returned = lax.all_to_all(
        outgoing.reshape(n * owners, rows, thin),
        ("dp", "expert"),
        split_axis=0,
        concat_axis=0,
        tiled=True,
    )

    scaled, gate, pre_grad = lax.optimization_barrier((scaled, gate, pre_grad))
    hidden_all = forward([scaled] * n)
    gate = reduced([gate[:, p] for p in range(n)])
    hidden_all, gate = lax.optimization_barrier((hidden_all, gate))
    gate_grad = gate.reshape(1, experts, cap)
    out_blocks = call(
        functools.partial(grad_out_kernel, n, cap),
        [((experts, share, quarter), BF16)] * n,
        [*hidden_all, up],
        scratch=[pltpu.VMEM((every, n * share), BF16)],
        flops=2 * every * quarter * n * share,
    )
    out_blocks = backward(out_blocks)

    own_grad = pre_grad[0].reshape(experts, n, cap, share).transpose(1, 0, 2, 3)
    own_grad = jnp.stack(turned(own_grad))
    w_in_grad = jnp.einsum("gecd,gecf->edf", inputs, own_grad, preferred_element_type=F32).astype(BF16)
    w_out_grad = jnp.zeros(w_out.shape, BF16)
    for s in range(n):
        w_out_grad = lax.dynamic_update_slice(w_out_grad, out_blocks[s], (0, 0, at(s) * quarter))

    mine = asked[:, :1]
    home = jnp.where(mine >= 0, mine + jnp.arange(n, dtype=jnp.int32)[None, :, None] * tok, -1)
    (token_grad,) = call(
        functools.partial(sum_kernel, n, tok),
        [((tok, width), BF16)],
        [home.reshape(1, owners * rows), returned.reshape(n, owners * rows, thin)],
        [whole((1, owners * rows)), pl.BlockSpec((1, owners * rows, thin), lambda q: (q, 0, 0))],
        [pl.BlockSpec((tok, quarter), lambda q: (0, q))],
        (n,),
        [pltpu.VMEM((n * tok, owners * rows), BF16)],
        flops=2 * n * tok * owners * rows * quarter,
    )
    return (token_grad[None], gate_grad, w_in_grad, w_out_grad)


def solution(mesh):
    return jax.shard_map(
        shards,
        mesh=mesh,
        in_specs=(
            P("dp", "expert", None),
            P("dp", "expert"),
            P("dp", "expert", None),
            P("dp", "expert", None),
            P("dp", "expert", None, None),
            P("expert", None, "dp"),
            P("expert", "dp", None),
        ),
        out_specs=(
            P("dp", "expert", None),
            P("dp", "expert", None),
            P("expert", None, "dp"),
            P("expert", "dp", None),
        ),
        check_vma=False,
    )
```

```python
import functools

import jax
import jax.numpy as jnp
from jax import lax
from jax.experimental import pallas as pl
from jax.experimental.pallas import tpu as pltpu
from jax.sharding import PartitionSpec as P

SQRT_HALF = 0.7071067811865476
INV_ROOT_TWO_PI = 0.3989422804014327
PEER = 6
F32 = jnp.float32
BF16 = jnp.bfloat16
VMEM_BYTES = 28 * 1024 * 1024


def dot(a, b, dims):
    return lax.dot_general(a, b, (dims, ((), ())), preferred_element_type=F32)


def whole(shape):
    return pl.BlockSpec(shape, lambda *_: (0,) * len(shape))


def call(kernel, outs, args, in_specs=None, out_specs=None, grid=(1,), scratch=(), flops=0, scalars=0):
    shapes = [jax.ShapeDtypeStruct(shape, dtype) for shape, dtype in outs]
    sizes = [a.size * a.dtype.itemsize for a in args]
    sizes += [s.size * s.dtype.itemsize for s in shapes]
    in_specs = in_specs or [whole(a.shape) for a in args[scalars:]]
    out_specs = out_specs or [whole(s.shape) for s in shapes]
    return pl.pallas_call(
        kernel,
        out_shape=shapes,
        grid_spec=pltpu.PrefetchScalarGridSpec(
            num_scalar_prefetch=scalars,
            grid=grid,
            in_specs=in_specs,
            out_specs=out_specs,
            scratch_shapes=list(scratch),
        ),
        compiler_params=pltpu.CompilerParams(vmem_limit_bytes=VMEM_BYTES),
        cost_estimate=pl.CostEstimate(flops=flops, bytes_accessed=sum(sizes), transcendentals=0),
    )(*args)


def column(rows):
    size = rows.shape[1]
    eye = lax.broadcasted_iota(jnp.int32, (size, size), 0) == lax.broadcasted_iota(jnp.int32, (size, size), 1)
    parts = [
        jnp.sum(jnp.where(eye, rows[k : k + 1], 0), axis=1, keepdims=True) for k in range(rows.shape[0])
    ]
    return jnp.concatenate(parts, axis=0)


def pack_kernel(n, tok, pick, *refs):
    blocks, sent, held = refs[:n], refs[n], refs[n + 1]

    @pl.when(pl.program_id(0) == 0)
    def _():
        for p in range(n):
            held[p * tok : (p + 1) * tok] = blocks[p][...]

    ids = lax.broadcasted_iota(jnp.int32, (pick.shape[0], n * tok), 1)
    onehot = jnp.where(pick[...] == ids, 1.0, 0.0).astype(BF16)
    sent[...] = dot(onehot, held[...], ((1,), (0,))).astype(BF16)


def project_kernel(n, cap, into, got, wide, up, *outs):
    share = wide.shape[1] // n
    ids = lax.broadcasted_iota(jnp.int32, (n * cap, got.shape[0]), 1)
    onehot = jnp.where(column(into[0]) == ids, 1.0, 0.0).astype(BF16)
    up[...] = dot(onehot, got[...], ((1,), (0,))).astype(BF16)
    part = dot(up[...], wide[0], ((1,), (1,)))
    for s in range(n):
        for p in range(n):
            low = ((p - s) % n) * cap
            block = part[p * cap : (p + 1) * cap, s * share : (s + 1) * share]
            outs[s][low : low + cap] = block.astype(outs[s].dtype)


def back_kernel(n, cap, me, place, *refs):
    ps, wide, out, tall, back = refs[:n], *refs[n:]
    experts, width, _ = wide.shape
    share = wide.shape[2] // n
    thin = width // n
    step = out.shape[1] // 2
    p = pl.program_id(0)

    @pl.when(p == 0)
    def _():
        for e in range(experts):
            for s in range(n):
                for g in range(n):
                    low = (e * n + (g - s) % n) * cap
                    tall[g * cap : (g + 1) * cap, s * share : (s + 1) * share] = ps[s][low : low + cap]
            mine = dot(tall[...], wide[e], ((1,), (1,))).astype(BF16)
            for g in range(n):
                back[g, e * cap : (e + 1) * cap] = mine[g * cap : (g + 1) * cap]

    owners = out.shape[1] // (n * PEER)
    ids = lax.broadcasted_iota(jnp.int32, (owners * 8, experts * cap), 0)
    onehot = jnp.where(ids == place[pl.ds(p, 1)], 1.0, 0.0).astype(BF16)
    full = dot(onehot, back[p], ((1,), (0,))).reshape(owners, 8, width)
    row = lax.broadcasted_iota(jnp.int32, (owners, 8, thin), 1)
    first = full[:, :, :thin]
    second = pltpu.roll(full[:, :, thin : 2 * thin], 6, 1)
    third = pltpu.roll(full[:, :, 2 * thin : 3 * thin], 4, 1)
    fourth = pltpu.roll(full[:, :, 3 * thin :], 2, 1)
    tiles = [
        jnp.where(row < 6, first, second),
        jnp.where(row < 4, second, third),
        jnp.where(row < 2, third, fourth),
    ]
    out[0] = jnp.concatenate(tiles, axis=1).reshape(owners * n * PEER, thin).astype(BF16)


def grad_out_kernel(n, cap, *refs):
    hs, up, outs, tall = refs[:n], refs[n], refs[n + 1 : 2 * n + 1], refs[2 * n + 1]
    experts, share, _ = outs[0].shape
    for s in range(n):
        for e in range(experts):
            for p in range(n):
                low = (e * n + (p - s) % n) * cap
                high = (e * n + p) * cap
                tall[high : high + cap, s * share : (s + 1) * share] = hs[s][low : low + cap]
    for e in range(experts):
        rows = slice(e * n * cap, (e + 1) * n * cap)
        grad = dot(tall[rows], up[rows], ((0,), (0,)))
        for s in range(n):
            outs[s][e] = grad[s * share : (s + 1) * share].astype(BF16)


def sum_kernel(n, tok, home, returned, out, onehot):
    rows, thin = returned.shape[1:]

    @pl.when(pl.program_id(0) == 0)
    def _():
        ids = lax.broadcasted_iota(jnp.int32, (n * tok, rows), 0)
        onehot[...] = jnp.where(home[...] == ids, 1.0, 0.0).astype(BF16)

    total = dot(onehot[...], returned[0], ((1,), (0,))).astype(BF16)
    for b in range(n):
        out[:, b * thin : (b + 1) * thin] = total[b * tok : (b + 1) * tok]


def shards(out_grad, count, chosen, gates, x_slots, w_in, w_out):
    tok = out_grad.shape[1]
    width = out_grad.shape[2]
    experts, cap = chosen.shape[1:]
    slots = experts * cap
    share = w_in.shape[2]
    n = lax.axis_size("dp")
    owners = lax.axis_size("expert")
    me = lax.axis_index("dp")
    quarter = width // n
    thin = quarter // n
    rows = n * PEER
    every = n * slots

    def shift(x, s):
        return lax.ppermute(x, "dp", [(a, (a + s) % n) for a in range(n)])

    def at(s):
        return lax.rem(me + (s + n), n)

    def columns(x, s):
        return lax.dynamic_slice_in_dim(x, at(s) * quarter, quarter, axis=x.ndim - 1)

    def forward(blocks):
        moved = {s: shift(blocks[s], s) for s in (2, 1, 3)}
        return [blocks[0]] + [moved[s] for s in range(1, n)]

    def backward(blocks):
        moved = {s: shift(blocks[s], -s) for s in (2, 1, 3)}
        return [blocks[0]] + [moved[s] for s in range(1, n)]

    def reduced(blocks):
        total = blocks[0]
        for block in backward(blocks)[1:]:
            total = total + block.astype(F32)
        return total

    inputs = lax.all_gather(x_slots.reshape(slots, width), "dp", axis=0, tiled=True)
    inputs = inputs.reshape(n, experts, cap, width)

    def turned(x):
        return [lax.dynamic_index_in_dim(x, at(-p), 0, keepdims=False) for p in range(n)]

    facts = jnp.stack([gates.reshape(slots), chosen.reshape(slots).astype(F32)])
    facts = jnp.stack(forward([facts] * n))
    tokens = facts[:, 1].astype(jnp.int32)
    source = lax.div(tokens, tok)
    onehot = (source[:, :, None] == jnp.arange(owners, dtype=jnp.int32)).astype(BF16)
    slot_ids = jnp.arange(slots, dtype=jnp.int32)
    earlier = (slot_ids[None, :] < slot_ids[:, None]).astype(BF16)
    before = jnp.einsum("st,ptk->psk", earlier, onehot, preferred_element_type=F32)
    rank = jnp.sum(before * onehot.astype(F32), axis=2).astype(jnp.int32)
    marked = rank[:, :, None] == jnp.arange(8, dtype=jnp.int32)
    marked = jnp.where(marked, (lax.rem(tokens, tok) + 1)[:, :, None], 0).astype(BF16)
    request = jnp.einsum("psk,psr->kpr", onehot, marked, preferred_element_type=F32)
    request = request.astype(jnp.int32).reshape(owners, n * 8) - 1
    asked = lax.all_to_all(request, "expert", split_axis=0, concat_axis=0, tiled=True)
    asked = asked.reshape(owners, n, 8)[:, :, :PEER]

    spread = jnp.maximum(count[0], 1).astype(F32)[:, None]
    table = (out_grad[0].astype(F32) / spread).astype(BF16)
    held = forward([columns(table, s) for s in range(n)])

    place = source * rows + rank
    scale = facts[:, 0].reshape(n, experts, cap).transpose(1, 0, 2).reshape(every, 1)
    into = place + jnp.arange(n, dtype=jnp.int32)[:, None] * PEER
    into = into.reshape(n, experts, cap).transpose(1, 0, 2)

    own_out = [columns(w_out, s) for s in range(n)]
    own_in = [lax.dynamic_slice_in_dim(w_in, at(s) * quarter, quarter, axis=1) for s in range(n)]
    w_out_all = forward(own_out)
    own_in, w_out_all = lax.optimization_barrier((own_in, w_out_all))
    w_in_all = forward(own_in)
    w_out_wide = jnp.concatenate(w_out_all, axis=1)
    inputs, w_in_all = lax.optimization_barrier((inputs, w_in_all))

    start = jnp.arange(n, dtype=jnp.int32)[None, :, None] * tok
    pick = jnp.where(asked >= 0, asked + start, -1).reshape(owners * rows, 1)
    (sent,) = call(
        functools.partial(pack_kernel, n, tok),
        [((owners * rows, quarter), BF16)],
        [pick, *held],
        [pl.BlockSpec((owners * rows // 6, 1), lambda t: (t, 0))] + [whole((tok, quarter))] * n,
        [pl.BlockSpec((owners * rows // 6, quarter), lambda t: (t, 0))],
        (6,),
        [pltpu.VMEM((n * tok, quarter), BF16)],
        flops=2 * owners * rows * n * tok * quarter,
    )
    got = lax.all_to_all(
        sent.reshape(owners, rows, quarter), "expert", split_axis=0, concat_axis=0, tiled=True
    )

    pre = jnp.einsum("gecd,edf->gecf", inputs, w_in, preferred_element_type=F32)
    pre, w_in_all = lax.optimization_barrier((pre, w_in_all))
    w_in_wide = jnp.concatenate(w_in_all, axis=2)
    pre = jnp.stack(turned(pre), 1).reshape(every, share)
    normal_cdf = 0.5 * (1.0 + lax.erf(pre * SQRT_HALF))
    slope = scale * (normal_cdf + pre * jnp.exp(-0.5 * pre * pre) * INV_ROOT_TWO_PI)
    hidden = pre * normal_cdf
    scaled = (scale * hidden).astype(BF16)
    hidden = hidden.astype(BF16)

    partials = [((every, share), F32)] + [((every, share), BF16)] * (n - 1)
    up, *partial = call(
        functools.partial(project_kernel, n, cap),
        [((every, quarter), BF16)] + partials,
        [into, got.reshape(owners * rows, quarter), w_out_wide],
        [pl.BlockSpec((1, n, cap), lambda e: (e, 0, 0)), whole((owners * rows, quarter))]
        + [pl.BlockSpec((1, n * share, quarter), lambda e: (e, 0, 0))],
        [pl.BlockSpec((n * cap, quarter), lambda e: (e, 0))]
        + [pl.BlockSpec((n * cap, share), lambda e: (e, 0))] * n,
        (experts,),
        flops=2 * every * quarter * (n * share + owners * rows),
    )
    project = reduced(partial)
    gate = jnp.sum(hidden.astype(F32) * project, axis=1).reshape(experts, n, cap)
    pre_grad = forward([(project * slope).astype(BF16)] * n)

    (outgoing,) = call(
        functools.partial(back_kernel, n, cap),
        [((n, owners * rows, thin), BF16)],
        [me.reshape(1), source * 8 + rank, *pre_grad, w_in_wide],
        out_specs=[
            pl.BlockSpec((1, owners * rows, thin), lambda p, m: (lax.rem(m[0] + n - p, n), 0, 0))
        ],
        grid=(n,),
        scratch=[
            pltpu.VMEM((n * cap, n * share), BF16),
            pltpu.VMEM((n, slots, quarter), BF16),
        ],
        flops=2 * every * quarter * (n * share + owners * rows),
        scalars=1,
    )
    returned = lax.all_to_all(
        outgoing.reshape(n * owners, rows, thin),
        ("dp", "expert"),
        split_axis=0,
        concat_axis=0,
        tiled=True,
    )

    scaled, gate, pre_grad = lax.optimization_barrier((scaled, gate, pre_grad))
    hidden_all = forward([scaled] * n)
    gate = reduced([gate[:, p] for p in range(n)])
    hidden_all, gate = lax.optimization_barrier((hidden_all, gate))
    gate_grad = gate.reshape(1, experts, cap)
    out_blocks = call(
        functools.partial(grad_out_kernel, n, cap),
        [((experts, share, quarter), BF16)] * n,
        [*hidden_all, up],
        scratch=[pltpu.VMEM((every, n * share), BF16)],
        flops=2 * every * quarter * n * share,
    )
    out_blocks = backward(out_blocks)

    own_grad = pre_grad[0].reshape(experts, n, cap, share).transpose(1, 0, 2, 3)
    own_grad = jnp.stack(turned(own_grad))
    w_in_grad = jnp.einsum("gecd,gecf->edf", inputs, own_grad, preferred_element_type=F32).astype(BF16)
    w_out_grad = jnp.zeros(w_out.shape, BF16)
    for s in range(n):
        w_out_grad = lax.dynamic_update_slice(w_out_grad, out_blocks[s], (0, 0, at(s) * quarter))

    mine = asked[:, :1]
    home = jnp.where(mine >= 0, mine + jnp.arange(n, dtype=jnp.int32)[None, :, None] * tok, -1)
    (token_grad,) = call(
        functools.partial(sum_kernel, n, tok),
        [((tok, width), BF16)],
        [home.reshape(1, owners * rows), returned.reshape(n, owners * rows, thin)],
        [whole((1, owners * rows)), pl.BlockSpec((1, owners * rows, thin), lambda q: (q, 0, 0))],
        [pl.BlockSpec((tok, quarter), lambda q: (0, q))],
        (n,),
        [pltpu.VMEM((n * tok, owners * rows), BF16)],
        flops=2 * n * tok * owners * rows * quarter,
    )
    return (token_grad[None], gate_grad, w_in_grad, w_out_grad)


def solution(mesh):
    return jax.shard_map(
        shards,
        mesh=mesh,
        in_specs=(
            P("dp", "expert", None),
            P("dp", "expert"),
            P("dp", "expert", None),
            P("dp", "expert", None),
            P("dp", "expert", None, None),
            P("expert", None, "dp"),
            P("expert", "dp", None),
        ),
        out_specs=(
            P("dp", "expert", None),
            P("dp", "expert", None),
            P("expert", None, "dp"),
            P("expert", "dp", None),
        ),
        check_vma=False,
    )
```
